256 devices in a mesh: fsdp: 64 (over x, z, core), group: 4 (over y).
Axes of the slice: x: 4, y: 4, z: 8, core: 2. Of those that a mesh axis runs over, the one named last changes fastest.
Arguments:
- weights: bfloat16 [16, 3072, 4096], P('group', 'fsdp')
- placement: int32 [4, 20], P('group'), may hold values from 0 to 15, as said below
Outputs:
- rollout_codes: bfloat16 [4, 16384, 5, 3072], P('group', 'fsdp')
- rollout_scales: float32 [4, 20, 24, 32], P('group')
The draws below stay inside these ranges and needn't reach their ends.
Inputs may be any that keep to these rules, and one draw needn't show every extreme that they name: `placement`: in each row of the table the first 16 slots name every expert once; the last 4 slots name replicas drawn from 4 experts of that row.
All inputs are finite; a program needn't handle non-finite values.
Results may differ from the reference program's by a relative error of at most 0.001.
Values may be sent and summed in bfloat16 or wider, within the bound.
A program may use at most 128 MiB of HBM per device.

```python
import math
import jax
import jax.numpy as jnp
from jax import lax

D = 4096
TILE = 128
HOT = 4
REPLICAS = 4
OWNERS = 4
ROWS = 3072
EXPERTS = 16
SLOTS = 20
GROUPS = 4


def draw_weights(key, part):
    key = jax.random.fold_in(key, 1)
    first, second, third = jax.random.split(key, 3)
    base = jax.random.normal(first, (EXPERTS, ROWS, D), jnp.float32)
    spread = math.log(10.0)
    row_scale = jnp.exp(jax.random.uniform(second, (EXPERTS, ROWS, 1), jnp.float32, 0.0, spread))
    col_scale = jnp.exp(jax.random.uniform(third, (EXPERTS, 1, D), jnp.float32, 0.0, spread))
    return (base * row_scale * col_scale * (0.1 * D ** (-0.5))).astype(jnp.bfloat16)


def draw_placement(key, part):
    key = jax.random.fold_in(key, 2)
    first, second = jax.random.split(key)
    row_keys = jax.random.split(first, GROUPS)
    orders = jax.vmap(lambda one_key: jax.random.permutation(one_key, EXPERTS))(row_keys).astype(jnp.int32)
    picks = jax.random.randint(second, (GROUPS, REPLICAS), 0, HOT).astype(jnp.int32)
    extra = jnp.take_along_axis(orders, picks, axis=1)
    return jnp.concatenate([orders, extra], axis=1).astype(jnp.int32)


def setup_inputs(seed: int = 0) -> dict:
    arg_keys = jax.random.split(jax.random.key(seed), 3)
    return {
        "weights": draw_weights(jax.random.fold_in(arg_keys[2], 71), 0),
        "placement": draw_placement(jax.random.fold_in(arg_keys[2], 71), 0),
    }


EPSILON = 1e-6


def one_expert(matrix):
    row_count, columns = matrix.shape
    blocks = jnp.abs(matrix.astype(jnp.float32)).reshape(row_count // TILE, TILE, columns // TILE, TILE)
    expert_max = jnp.max(blocks, axis=(1, 3))
    scaled = matrix.astype(jnp.float32).reshape(row_count // TILE, TILE, columns // TILE, TILE) / (expert_max[:, None, :, None] + EPSILON)
    return scaled.astype(jnp.bfloat16).reshape(row_count, columns), expert_max


def reference(weights, placement):
    code_tiles, tile_max = lax.map(one_expert, weights)
    chosen = jnp.take(code_tiles, placement.astype(jnp.int32), axis=0)
    groups_all = chosen.shape[0]
    chosen = chosen.reshape(groups_all, OWNERS, SLOTS // OWNERS, ROWS, D)
    chosen = jnp.transpose(chosen, (0, 1, 4, 2, 3))
    rollout_codes = chosen.reshape(groups_all, OWNERS * D, SLOTS // OWNERS, ROWS)
    rollout_scales = jnp.take(tile_max, placement.astype(jnp.int32), axis=0)
    return rollout_codes, rollout_scales
```

```python
import functools

import jax
import jax.numpy as jnp
from jax import lax
from jax.experimental import pallas as pl
from jax.experimental.pallas import tpu as pltpu
from jax.sharding import PartitionSpec as P

MESH = pl.DeviceIdType.MESH
TILE = 128
EPSILON = 1e-6
NX, NY, NZ = 4, 4, 8
NC = 16
EXPERTS_HERE = 4
SLOTS_OWN = 5
ROWS_HERE = 48
ROW_TILES = 6
CHUNKS = 2 * ROW_TILES
Z_ORDER = [(0, 1)] + [(dz, dc) for dz in (1, 7, 2, 6, 3, 5, 4) for dc in (0, 1)]
X_ORDER = (2, 1, 3)
Y_ORDER = (2, 1, 3)


def comm_kernel(w_ref, place_ref, out_ref, scales_ref, *scratch):
    ybufs = scratch[:CHUNKS]
    (zbuf, staged, acc, zmax, ymax, xmax,
     z_send, z_recv, y_send, y_recv, x_send, x_recv, own_sem,
     sz_send, sz_recv, sy_send, sy_recv, sx_send, sx_recv) = scratch[CHUNKS:]
    f = lax.axis_index("fsdp")
    y = lax.axis_index("group")
    x = f // NC
    c = f % NC
    z = c // 2
    core = c % 2

    def z_dev(step):
        dz, dc = step
        return 2 * ((z + dz) % NZ) + (core + dc) % 2

    def y_dev(dy):
        return (y + dy) % NY

    def x_dev(dx):
        return (x + dx) % NX

    barrier = pltpu.get_barrier_semaphore()
    for step in Z_ORDER:
        pl.semaphore_signal(barrier, inc=1, device_id=(x * NC + z_dev(step), y), device_id_type=MESH)
    for d in Y_ORDER:
        pl.semaphore_signal(barrier, inc=1, device_id=(f, y_dev(d)), device_id_type=MESH)
    for d in X_ORDER:
        pl.semaphore_signal(barrier, inc=1, device_id=(x_dev(d) * NC + c, y), device_id_type=MESH)
    pl.semaphore_wait(barrier, len(Z_ORDER) + len(Y_ORDER) + len(X_ORDER))

    waits = []

    def z_copy(k, ct):
        to = z_dev(Z_ORDER[k])
        cols = pl.ds(pl.multiple_of(to * (2 * TILE) + ct * TILE, TILE), TILE)
        rows = pl.ds(pl.multiple_of(c * ROWS_HERE, 16), ROWS_HERE)
        return pltpu.make_async_remote_copy(
            src_ref=w_ref.at[:, :, cols],
            dst_ref=zbuf.at[ct, :, rows, :],
            send_sem=z_send.at[ct, k],
            recv_sem=z_recv.at[ct, c],
            device_id=(x * NC + to, y),
            device_id_type=MESH,
        )

    def z_start(k, ct):
        copy = z_copy(k, ct)
        copy.start()
        waits.append(copy)

    for ct in range(2):
        cols = pl.ds(pl.multiple_of(c * (2 * TILE) + ct * TILE, TILE), TILE)
        rows = pl.ds(pl.multiple_of(c * ROWS_HERE, 16), ROWS_HERE)
        pltpu.make_async_copy(w_ref.at[:, :, cols], zbuf.at[ct, :, rows, :], z_recv.at[ct, c]).start()
        for k in range(5):
            z_start(k, ct)
    for k in range(5, len(Z_ORDER)):
        for ct in range(2):
            z_start(k, ct)

    def z_wait(ct, first, last):
        def body(s, carry):
            rows = pl.ds(pl.multiple_of(s * ROWS_HERE, 16), ROWS_HERE)
            part = zbuf.at[ct, :, rows, :]
            pltpu.make_async_copy(part, part, z_recv.at[ct, s]).wait()
            return carry

        lax.fori_loop(first, last, body, 0)

    tile0 = (3 * z) // 4

    def tile_of(i):
        return (tile0 + i // 2) % ROW_TILES

    def first_source(t):
        return (8 * t) // 3

    def end_source(t):
        return (8 * t + 7) // 3 + 1

    acc[...] = jnp.zeros_like(acc)
    lane = lax.broadcasted_iota(jnp.int32, acc.shape, 1)
    sub = lax.broadcasted_iota(jnp.int32, acc.shape, 0)

    def y_copy(i, n):
        here = pl.ds(y * EXPERTS_HERE, EXPERTS_HERE)
        return pltpu.make_async_remote_copy(
            src_ref=ybufs[i].at[here],
            dst_ref=ybufs[i].at[here],
            send_sem=y_send.at[i, n],
            recv_sem=y_recv.at[i, n],
            device_id=(f, y_dev(Y_ORDER[n])),
            device_id_type=MESH,
        )

    def scale_and_send(i):
        order, ct = i // 2, i % 2
        t = tile_of(i)
        first, last = first_source(t), end_source(t)
        if order > 0:
            first = jnp.where(t > 0, jnp.maximum(first, end_source(t - 1)), first)
        if order == ROW_TILES - 1:
            last = jnp.where(t + 1 == tile0, jnp.minimum(last, first_source(tile0)), last)
        z_wait(ct, first, last)
        rows = pl.ds(pl.multiple_of(t * TILE, TILE), TILE)
        total = acc[...]
        for e in range(EXPERTS_HERE):
            block = zbuf[ct, e, rows, :].astype(jnp.float32)
            top = jnp.max(jnp.max(jnp.abs(block), axis=0, keepdims=True), axis=1, keepdims=True)
            code = (block / (top + EPSILON)).astype(jnp.bfloat16)
            ybufs[i][y * EXPERTS_HERE + e] = code.T
            at = (sub == t) & (lane == e * 32 + 2 * c + ct)
            total = jnp.where(at, top, total)
        acc[...] = total
        for n in range(3):
            copy = y_copy(i, n)
            copy.start()
            waits.append(copy)

    def select_and_send(i):
        ct = i % 2
        t = tile_of(i)
        for n, d in enumerate(Y_ORDER):
            there = pl.ds(((y - d) % NY) * EXPERTS_HERE, EXPERTS_HERE)
            part = ybufs[i].at[there]
            pltpu.make_async_copy(part, part, y_recv.at[i, n]).wait()
        for n, d in enumerate(X_ORDER + (0,)):
            owner = x_dev(d)
            for j in range(SLOTS_OWN):
                expert = place_ref[0, owner * SLOTS_OWN + j]
                staged[i, n, j] = ybufs[i][expert]
            target = out_ref.at[x * ROW_TILES + t, ct]
            if d:
                copy = pltpu.make_async_remote_copy(
                    src_ref=staged.at[i, n],
                    dst_ref=target,
                    send_sem=x_send.at[i, n],
                    recv_sem=x_recv.at[i, n],
                    device_id=(owner * NC + c, y),
                    device_id_type=MESH,
                )
                copy.start()
                waits.append(copy)
            else:
                pltpu.make_async_copy(staged.at[i, n], target, own_sem.at[i]).start()

    for i in range(CHUNKS + 1):
        if i < CHUNKS:
            scale_and_send(i)
        if i >= 1:
            select_and_send(i - 1)

    zmax[c] = acc[...]
    for k, step in enumerate(Z_ORDER):
        pltpu.make_async_remote_copy(
            src_ref=zmax.at[c], dst_ref=zmax.at[c], send_sem=sz_send.at[k], recv_sem=sz_recv.at[c],
            device_id=(x * NC + z_dev(step), y), device_id_type=MESH,
        ).start()
    for k, step in enumerate(Z_ORDER):
        source = z_dev(step)
        part = zmax.at[source]
        pltpu.make_async_copy(part, part, sz_recv.at[source]).wait()
        pltpu.make_async_copy(part, part, sz_send.at[k]).wait()
    ymax[y] = jnp.max(zmax[...], axis=0)
    for n, d in enumerate(Y_ORDER):
        pltpu.make_async_remote_copy(
            src_ref=ymax.at[y], dst_ref=ymax.at[y], send_sem=sy_send.at[n], recv_sem=sy_recv.at[n],
            device_id=(f, y_dev(d)), device_id_type=MESH,
        ).start()
    for n, d in enumerate(Y_ORDER):
        part = ymax.at[(y - d) % NY]
        pltpu.make_async_copy(part, part, sy_recv.at[n]).wait()
        pltpu.make_async_copy(part, part, sy_send.at[n]).wait()
    xmax[x] = ymax[...]
    for n, d in enumerate(X_ORDER):
        pltpu.make_async_remote_copy(
            src_ref=xmax.at[x], dst_ref=xmax.at[x], send_sem=sx_send.at[n], recv_sem=sx_recv.at[n],
            device_id=(x_dev(d) * NC + c, y), device_id_type=MESH,
        ).start()
    for n, d in enumerate(X_ORDER):
        part = xmax.at[(x - d) % NX]
        pltpu.make_async_copy(part, part, sx_recv.at[n]).wait()
        pltpu.make_async_copy(part, part, sx_send.at[n]).wait()
    scales_ref[...] = xmax[...]

    for copy in waits:
        copy.wait_send()
    for i in range(CHUNKS):
        ct = i % 2
        t = tile_of(i)
        for n, d in enumerate(X_ORDER):
            part = out_ref.at[((x - d) % NX) * ROW_TILES + t, ct]
            pltpu.make_async_copy(part, part, x_recv.at[i, n]).wait()
        mine = out_ref.at[x * ROW_TILES + t, ct]
        pltpu.make_async_copy(staged.at[i, 3], mine, own_sem.at[i]).wait()


def exchange(weights, placement):
    sem = pltpu.SemaphoreType.DMA
    return pl.pallas_call(
        comm_kernel,
        out_shape=(
            jax.ShapeDtypeStruct((NX * ROW_TILES, 2, SLOTS_OWN, TILE, TILE), jnp.bfloat16),
            jax.ShapeDtypeStruct((NX, NY, 8, TILE), jnp.float32),
        ),
        in_specs=[pl.BlockSpec(memory_space=pl.ANY), pl.BlockSpec(memory_space=pltpu.SMEM)],
        out_specs=(pl.BlockSpec(memory_space=pl.ANY), pl.BlockSpec(memory_space=pltpu.VMEM)),
        scratch_shapes=[pltpu.VMEM((16, TILE, TILE), jnp.bfloat16)] * CHUNKS
        + [
            pltpu.VMEM((2, EXPERTS_HERE, ROW_TILES * TILE, TILE), jnp.bfloat16),
            pltpu.VMEM((CHUNKS, 4, SLOTS_OWN, TILE, TILE), jnp.bfloat16),
            pltpu.VMEM((8, TILE), jnp.float32),
            pltpu.VMEM((NC, 8, TILE), jnp.float32),
            pltpu.VMEM((NY, 8, TILE), jnp.float32),
            pltpu.VMEM((NX, NY, 8, TILE), jnp.float32),
            sem((2, 15)), sem((2, NC)),
            sem((CHUNKS, 3)), sem((CHUNKS, 3)),
            sem((CHUNKS, 3)), sem((CHUNKS, 3)), sem((CHUNKS,)),
            sem((15,)), sem((NC,)),
            sem((3,)), sem((3,)),
            sem((3,)), sem((3,)),
        ],
        compiler_params=pltpu.CompilerParams(
            collective_id=0, has_side_effects=True, vmem_limit_bytes=48 * 2**20
        ),
        name="reshard",
    )(weights, placement)


KB = 32


def weave_kernel(place_ref, parts_ref, maxima_ref, out_ref, scales_ref, spread):
    @pl.when(pl.program_id(0) == 0)
    def _():
        row = lax.broadcasted_iota(jnp.int32, spread.shape, 0)
        col = lax.broadcasted_iota(jnp.int32, spread.shape, 1)
        hit = (row // 8 == col % KB) & (row % 8 == col // KB)
        spread[...] = jnp.where(hit, 1.0, 0.0).astype(jnp.bfloat16)
        for s in range(20):
            expert = place_ref[0, s]
            table = maxima_ref[:, expert // 4]
            which = expert % 4
            part = table[:, :, :32]
            for e in range(1, 4):
                part = jnp.where(which == e, table[:, :, 32 * e:32 * (e + 1)], part)
            for q in range(NX):
                scales_ref[0, s, ROW_TILES * q:ROW_TILES * (q + 1), :] = part[q, :ROW_TILES]

    for q in range(NX * ROW_TILES // 2):
        left = parts_ref[2 * q, 0].reshape(SLOTS_OWN * KB, TILE)
        right = parts_ref[2 * q + 1, 0].reshape(SLOTS_OWN * KB, TILE)
        both = jnp.concatenate([left, right], axis=1)
        woven = jnp.dot(spread[...], both, preferred_element_type=jnp.float32)
        woven = woven.reshape(KB, 8, 2 * TILE)[:, :SLOTS_OWN, :].astype(jnp.bfloat16)
        out_ref[0, :, :, pl.ds(q * 2 * TILE, 2 * TILE)] = woven


def weave(placement, parts, maxima):
    steps = 2 * TILE // KB
    per_tile = TILE // KB
    return pl.pallas_call(
        weave_kernel,
        out_shape=(
            jax.ShapeDtypeStruct((1, 2 * TILE, SLOTS_OWN, NX * ROW_TILES * TILE), jnp.bfloat16),
            jax.ShapeDtypeStruct((1, 20, NX * ROW_TILES, 32), jnp.float32),
        ),
        grid=(steps,),
        in_specs=[
            pl.BlockSpec(memory_space=pltpu.SMEM),
            pl.BlockSpec(
                (NX * ROW_TILES, 1, SLOTS_OWN, KB, TILE), lambda i: (0, i // per_tile, 0, i % per_tile, 0)
            ),
            pl.BlockSpec((NX, NY, 8, TILE), lambda i: (0, 0, 0, 0)),
        ],
        out_specs=(
            pl.BlockSpec((1, KB, SLOTS_OWN, NX * ROW_TILES * TILE), lambda i: (0, i, 0, 0)),
            pl.BlockSpec((1, 20, NX * ROW_TILES, 32), lambda i: (0, 0, 0, 0)),
        ),
        scratch_shapes=[pltpu.VMEM((8 * KB, SLOTS_OWN * KB), jnp.bfloat16)],
        compiler_params=pltpu.CompilerParams(vmem_limit_bytes=48 * 2**20),
        name="weave",
    )(placement, parts, maxima)


def on_device(weights, placement):
    parts, maxima = exchange(weights, placement)
    return weave(placement, parts, maxima)


def solution(mesh):
    in_specs = (P("group", "fsdp", None), P("group", None))
    out_specs = (P("group", "fsdp", None, None), P("group", None, None, None))
    return jax.shard_map(
        on_device, mesh=mesh, in_specs=in_specs, out_specs=out_specs, check_vma=False
    )
```

```python
import jax
import jax.numpy as jnp
from jax import lax
from jax.experimental import pallas as pl
from jax.experimental.pallas import tpu as pltpu
from jax.sharding import PartitionSpec as P

MESH = pl.DeviceIdType.MESH
TILE = 128
EPSILON = 1e-6
NX, NY, NZ = 4, 4, 8
NC = 16
EXPERTS_HERE = 4
SLOTS_OWN = 5
SLOTS = 20
ROWS_HERE = 48
ROW_TILES = 6
CHUNKS = 2 * ROW_TILES
SHARED = {10: 1, 11: -1}
GATHERS = CHUNKS + len(SHARED)
DIRECT = tuple(range(14))
SCHEDULE = (
    "c0", "o0", "n1", "h1", "z5", "z6", "c1", "s0", "o1", "h2", "c2", "z7", "z8", "s1", "o2", "c3",
    "o3", "h3", "z9", "z10", "s2", "z11", "z12", "c4", "o4", "s3", "z13", "z14", "c5", "o5", "s4",
    "c6", "o6", "c10", "c11", "s5", "c7", "o7", "s6", "c8", "o8", "r10", "s7", "c9", "o9", "r11",
    "s8", "o10", "o11", "mz", "s9", "s10", "my", "s11", "mx", "md",
)
Z_ORDER = [(0, 1)] + [(dz, dc) for dz in (7, 1, 6, 5, 4, 3, 2) for dc in (0, 1)]
X_ORDER = (2, 1, 3)
NEAR = 5
Y_ORDER = (2, 1, 3)


def block_of(out_ref, x, t, ct):
    rows = pl.ds(pl.multiple_of((x * ROW_TILES + t) * TILE, TILE), TILE)
    return out_ref.at[:, pl.ds(ct * TILE, TILE), rows]


def comm_kernel(w_hbm, place_ref, out_ref, maxima_ref, *scratch):
    ybufs = scratch[:GATHERS]
    (w_ref, w_sem, zbuf, staged, acc, zmax, ymax, xmax,
     z_send, z_recv, y_send, y_recv, x_send, x_recv, own_sem,
     sz_send, sz_recv, sy_send, sy_recv, sx_send, sx_recv, up_sem, down_sem) = scratch[GATHERS:]
    f = lax.axis_index("fsdp")
    y = lax.axis_index("group")
    x = f // NC
    c = f % NC
    z = c // 2
    core = c % 2

    def z_dev(step):
        dz, dc = step
        return 2 * ((z + dz) % NZ) + (core + dc) % 2

    def y_dev(dy):
        return (y + dy) % NY

    def x_dev(dx):
        return (x + dx) % NX

    fetch = pltpu.make_async_copy(w_hbm, w_ref, w_sem)
    fetch.start()
    barrier = pltpu.get_barrier_semaphore()
    for step in Z_ORDER[:NEAR]:
        pl.semaphore_signal(barrier, inc=1, device_id=(x * NC + z_dev(step), y), device_id_type=MESH)
    for d in Y_ORDER:
        pl.semaphore_signal(barrier, inc=1, device_id=(f, y_dev(d)), device_id_type=MESH)
    for d in X_ORDER:
        pl.semaphore_signal(barrier, inc=1, device_id=(x_dev(d) * NC + c, y), device_id_type=MESH)
    pl.semaphore_wait(barrier, NEAR + len(Y_ORDER) + len(X_ORDER))

    fetch.wait()
    waits = []

    def relay(level):
        if level:
            pl.semaphore_wait(up_sem.at[level - 1], 1)
            pl.semaphore_wait(down_sem.at[level - 1], 1)
        if level < 3:
            for dz, told in ((1, up_sem), (-1, down_sem)):
                pl.semaphore_signal(
                    told.at[level], inc=1, device_id=(x * NC + z_dev((dz, 0)), y), device_id_type=MESH
                )

    relay(0)
    def z_copy(k, ct):
        to = z_dev(Z_ORDER[k])
        cols = pl.ds(pl.multiple_of(to * (2 * TILE) + ct * TILE, TILE), TILE)
        rows = pl.ds(pl.multiple_of(c * ROWS_HERE, 16), ROWS_HERE)
        return pltpu.make_async_remote_copy(
            src_ref=w_ref.at[:, :, cols],
            dst_ref=zbuf.at[ct, :, rows, :],
            send_sem=z_send.at[ct, k],
            recv_sem=z_recv.at[ct, c],
            device_id=(x * NC + to, y),
            device_id_type=MESH,
        )

    def z_start(k, ct):
        copy = z_copy(k, ct)
        copy.start()
        waits.append(copy)

    for ct in range(2):
        cols = pl.ds(pl.multiple_of(c * (2 * TILE) + ct * TILE, TILE), TILE)
        rows = pl.ds(pl.multiple_of(c * ROWS_HERE, 16), ROWS_HERE)
        pltpu.make_async_copy(w_ref.at[:, :, cols], zbuf.at[ct, :, rows, :], z_recv.at[ct, c]).start()
    for k in range(5):
        z_start(k, 0)

    def z_wait(ct, first, last):
        def body(s, carry):
            rows = pl.ds(pl.multiple_of(s * ROWS_HERE, 16), ROWS_HERE)
            part = zbuf.at[ct, :, rows, :]
            pltpu.make_async_copy(part, part, z_recv.at[ct, s]).wait()
            return carry

        lax.fori_loop(first, last, body, 0)

    tile0 = (3 * z) // 4

    def tile_of(i):
        return (tile0 + i // 2) % ROW_TILES

    def first_source(t):
        return (8 * t) // 3

    def end_source(t):
        return (8 * t + 7) // 3 + 1

    acc[...] = jnp.zeros_like(acc)
    lane = lax.broadcasted_iota(jnp.int32, acc.shape, 1)
    sub = lax.broadcasted_iota(jnp.int32, acc.shape, 0)

    def shared_gather(i):
        return CHUNKS + sorted(SHARED).index(i)

    def experts_of(dy, first=0, count=EXPERTS_HERE):
        return pl.ds(y_dev(dy) * EXPERTS_HERE + first, count)

    def y_copy(g, n, to, experts):
        copy = pltpu.make_async_remote_copy(
            src_ref=ybufs[g].at[experts],
            dst_ref=ybufs[g].at[experts],
            send_sem=y_send.at[g, n],
            recv_sem=y_recv.at[g, n],
            device_id=(f, y_dev(to)),
            device_id_type=MESH,
        )
        copy.start()
        waits.append(copy)

    def y_wait(g, n, experts):
        part = ybufs[g].at[experts]
        pltpu.make_async_copy(part, part, y_recv.at[g, n]).wait()

    def y_spread(g):
        if g in DIRECT:
            y_copy(g, 2, 2, experts_of(0))
        y_copy(g, 0, 1, experts_of(0))
        y_copy(g, 1, -1, experts_of(0))

    def y_forward(g):
        if g in DIRECT:
            return
        y_wait(g, 0, experts_of(-1))
        y_copy(g, 2, 1, experts_of(-1, 0, 2))
        y_wait(g, 1, experts_of(1))
        y_copy(g, 3, -1, experts_of(1, 2, 2))

    def y_finish(g):
        if g in DIRECT:
            y_wait(g, 0, experts_of(-1))
            y_wait(g, 1, experts_of(1))
            y_wait(g, 2, experts_of(2))
        else:
            y_wait(g, 2, experts_of(2, 0, 2))
            y_wait(g, 3, experts_of(2, 2, 2))

    def share_copy(i):
        g = shared_gather(i)
        return pltpu.make_async_remote_copy(
            src_ref=ybufs[i].at[experts_of(0)],
            dst_ref=ybufs[g].at[experts_of(0)],
            send_sem=x_send.at[i, 2],
            recv_sem=x_recv.at[i, 2],
            device_id=(x_dev(SHARED[i]) * NC + c, y),
            device_id_type=MESH,
        )

    seen = set()

    def scale(i):
        order, ct = i // 2, i % 2
        t = tile_of(i)
        first, last = first_source(t), end_source(t)
        if ((order - 1) % ROW_TILES, ct) in seen:
            first = jnp.where(t > 0, jnp.maximum(first, end_source(t - 1)), first)
        if ((order + 1) % ROW_TILES, ct) in seen:
            last = jnp.where(t < ROW_TILES - 1, jnp.minimum(last, first_source(t + 1)), last)
        seen.add((order, ct))
        z_wait(ct, first, last)
        rows = pl.ds(pl.multiple_of(t * TILE, TILE), TILE)
        total = acc[...]
        for e in range(EXPERTS_HERE):
            block = zbuf[ct, e, rows, :].astype(jnp.float32)
            top = jnp.max(jnp.max(jnp.abs(block), axis=0, keepdims=True), axis=1, keepdims=True)
            code = (block / (top + EPSILON)).astype(jnp.bfloat16)
            ybufs[i][y * EXPERTS_HERE + e] = code.T
            at = (sub == t) & (lane == e * 32 + 2 * c + ct)
            total = jnp.where(at, top, total)
        acc[...] = total
        if i in SHARED:
            copy = share_copy(i)
            copy.start()
            waits.append(copy)

    def spread_shared(i):
        g = shared_gather(i)
        part = ybufs[g].at[experts_of(0)]
        pltpu.make_async_copy(part, part, x_recv.at[i, 2]).wait()
        y_spread(g)

    def select(i, n, g, owner):
        for j in range(SLOTS_OWN):
            expert = place_ref[0, owner * SLOTS_OWN + j]
            staged[i, n, j] = ybufs[g][expert]

    def x_copy(i, n, rows_of, owner):
        copy = pltpu.make_async_remote_copy(
            src_ref=staged.at[i, n],
            dst_ref=block_of(out_ref, rows_of, tile_of(i), i % 2),
            send_sem=x_send.at[i, n],
            recv_sem=x_recv.at[i, n],
            device_id=(owner * NC + c, y),
            device_id_type=MESH,
        )
        copy.start()
        waits.append(copy)

    def own_copy(i, n, k, rows_of):
        return pltpu.make_async_copy(
            staged.at[i, n], block_of(out_ref, rows_of, tile_of(i), i % 2), own_sem.at[i, k]
        )

    def select_and_send(i):
        y_finish(i)
        if i in SHARED:
            g, d = shared_gather(i), SHARED[i]
            select(i, 1, i, x_dev(-d))
            x_copy(i, 1, x, x_dev(-d))
            y_finish(g)
            select(i, 0, g, x_dev(d))
            x_copy(i, 0, x_dev(-d), x_dev(d))
            select(i, 2, i, x)
            own_copy(i, 2, 0, x).start()
            select(i, 3, g, x)
            own_copy(i, 3, 1, x_dev(-d)).start()
        else:
            for n, d in enumerate(X_ORDER):
                select(i, n, i, x_dev(d))
                x_copy(i, n, x, x_dev(d))
            select(i, 3, i, x)
            own_copy(i, 3, 0, x).start()

    def maxima_copy(ref, here, to, send, recv):
        return pltpu.make_async_remote_copy(
            src_ref=ref.at[here], dst_ref=ref.at[here], send_sem=send, recv_sem=recv,
            device_id=to, device_id_type=MESH,
        )

    def maxima_wait(ref, source, recv):
        part = ref.at[source]
        pltpu.make_async_copy(part, part, recv).wait()

    def maxima_z_send():
        zmax[c] = acc[...]
        for k, step in enumerate(Z_ORDER):
            copy = maxima_copy(zmax, c, (x * NC + z_dev(step), y), sz_send.at[k], sz_recv.at[c])
            copy.start()
            waits.append(copy)

    def maxima_y_send():
        for k, step in enumerate(Z_ORDER):
            maxima_wait(zmax, z_dev(step), sz_recv.at[z_dev(step)])
        ymax[y] = jnp.max(zmax[...], axis=0)
        for n, d in enumerate(Y_ORDER):
            copy = maxima_copy(ymax, y, (f, y_dev(d)), sy_send.at[n], sy_recv.at[n])
            copy.start()
            waits.append(copy)

    def maxima_x_send():
        for n, d in enumerate(Y_ORDER):
            maxima_wait(ymax, (y - d) % NY, sy_recv.at[n])
        xmax[x] = ymax[...]
        for n, d in enumerate(X_ORDER):
            copy = maxima_copy(xmax, x, (x_dev(d) * NC + c, y), sx_send.at[n], sx_recv.at[n])
            copy.start()
            waits.append(copy)

    def maxima_done():
        for n, d in enumerate(X_ORDER):
            maxima_wait(xmax, (x - d) % NX, sx_recv.at[n])
        maxima_ref[...] = xmax[...]

    for step in SCHEDULE:
        if step == "mz":
            maxima_z_send()
        elif step == "my":
            maxima_y_send()
        elif step == "mx":
            maxima_x_send()
        elif step == "md":
            maxima_done()
        else:
            act, i = step[0], int(step[1:])
            if act == "h":
                relay(i)
            elif act == "n":
                for k in range(5):
                    z_start(k, 1)
            elif act == "z":
                for ct in range(2):
                    z_start(i, ct)
            elif act == "c":
                scale(i)
            elif act == "o":
                y_spread(i)
            elif act == "r":
                spread_shared(i)
            elif act == "f":
                y_forward(i)
            elif act == "g":
                y_forward(shared_gather(i))
            else:
                select_and_send(i)

    for copy in waits:
        copy.wait_send()
    def x_wait(i, n, rows_of):
        part = block_of(out_ref, rows_of, tile_of(i), i % 2)
        pltpu.make_async_copy(part, part, x_recv.at[i, n]).wait()

    for i in range(CHUNKS):
        if i in SHARED:
            d = SHARED[i]
            x_wait(i, 1, x_dev(d))
            x_wait(i, 0, x_dev(2))
            own_copy(i, 2, 0, x).wait()
            own_copy(i, 3, 1, x_dev(-d)).wait()
        else:
            for n, d in enumerate(X_ORDER):
                x_wait(i, n, x_dev(-d))
            own_copy(i, 3, 0, x).wait()


def exchange(weights, placement):
    sem = pltpu.SemaphoreType.DMA
    return pl.pallas_call(
        comm_kernel,
        out_shape=(
            pltpu.VMEM((SLOTS_OWN, 2 * TILE, NX * ROW_TILES * TILE), jnp.bfloat16),
            pltpu.VMEM((NX, NY, 8, TILE), jnp.float32),
        ),
        in_specs=[pl.BlockSpec(memory_space=pltpu.HBM), pl.BlockSpec(memory_space=pltpu.SMEM)],
        out_specs=(pl.BlockSpec(memory_space=pltpu.VMEM), pl.BlockSpec(memory_space=pltpu.VMEM)),
        scratch_shapes=[pltpu.VMEM((16, TILE, TILE), jnp.bfloat16)] * GATHERS
        + [
            pltpu.VMEM((EXPERTS_HERE, ROWS_HERE, 2 * TILE * NC), jnp.bfloat16),
            sem,
            pltpu.VMEM((2, EXPERTS_HERE, ROW_TILES * TILE, TILE), jnp.bfloat16),
            pltpu.VMEM((CHUNKS, 4, SLOTS_OWN, TILE, TILE), jnp.bfloat16),
            pltpu.VMEM((8, TILE), jnp.float32),
            pltpu.VMEM((NC, 8, TILE), jnp.float32),
            pltpu.VMEM((NY, 8, TILE), jnp.float32),
            pltpu.VMEM((NX, NY, 8, TILE), jnp.float32),
            sem((2, 15)), sem((2, NC)),
            sem((GATHERS, 4)), sem((GATHERS, 4)),
            sem((CHUNKS, 3)), sem((CHUNKS, 3)), sem((CHUNKS, 2)),
            sem((15,)), sem((NC,)),
            sem((3,)), sem((3,)),
            sem((3,)), sem((3,)),
            pltpu.SemaphoreType.REGULAR((3,)), pltpu.SemaphoreType.REGULAR((3,)),
        ],
        compiler_params=pltpu.CompilerParams(
            collective_id=0, has_side_effects=True, vmem_limit_bytes=40 * 2**20
        ),
        name="reshard",
    )(weights, placement)


PIECES = 8


def finish_kernel(place_ref, codes_ref, maxima_ref, out_ref, scales_ref, sems):
    rows = 2 * TILE // PIECES
    copies = []
    for q in range(PIECES):
        part = pl.ds(q * rows, rows)
        copy = pltpu.make_async_copy(codes_ref.at[:, part], out_ref.at[:, part], sems.at[q])
        copy.start()
        copies.append(copy)
    for s in range(SLOTS):
        expert = place_ref[0, s]
        which = expert % EXPERTS_HERE
        table = maxima_ref[:, expert // EXPERTS_HERE]
        part = table[:, :, :32]
        for e in range(1, EXPERTS_HERE):
            part = jnp.where(which == e, table[:, :, 32 * e:32 * (e + 1)], part)
        for q in range(NX):
            scales_ref[0, s, ROW_TILES * q:ROW_TILES * (q + 1), :] = part[q, :ROW_TILES]
    for copy in copies:
        copy.wait()


def finish(placement, codes, maxima):
    return pl.pallas_call(
        finish_kernel,
        out_shape=(
            jax.ShapeDtypeStruct(codes.shape, codes.dtype),
            jax.ShapeDtypeStruct((1, SLOTS, NX * ROW_TILES, 32), jnp.float32),
        ),
        in_specs=[
            pl.BlockSpec(memory_space=pltpu.SMEM),
            pl.BlockSpec(memory_space=pl.ANY),
            pl.BlockSpec(memory_space=pltpu.VMEM),
        ],
        out_specs=(pl.BlockSpec(memory_space=pl.ANY), pl.BlockSpec(memory_space=pltpu.VMEM)),
        scratch_shapes=[pltpu.SemaphoreType.DMA((PIECES,))],
        compiler_params=pltpu.CompilerParams(vmem_limit_bytes=16 * 2**20),
        name="finish",
    )(placement, codes, maxima)


def on_device(weights, placement):
    weights = pltpu.with_memory_space_constraint(weights, pltpu.HBM)
    placement = pltpu.with_memory_space_constraint(placement, pltpu.HBM)
    codes, maxima = exchange(weights, placement)
    codes, scales = finish(placement, codes, maxima)
    return jnp.transpose(codes, (1, 0, 2))[None], scales


def solution(mesh):
    in_specs = (P("group", "fsdp", None), P("group", None))
    out_specs = (P("group", "fsdp", None, None), P("group", None, None, None))
    return jax.shard_map(
        on_device, mesh=mesh, in_specs=in_specs, out_specs=out_specs, check_vma=False
    )
```

```python
import jax
import jax.numpy as jnp
from jax import lax
from jax.experimental import pallas as pl
from jax.experimental.pallas import tpu as pltpu
from jax.sharding import PartitionSpec as P

MESH = pl.DeviceIdType.MESH
TILE = 128
EPSILON = 1e-6
NX, NY, NZ = 4, 4, 8
NC = 16
EXPERTS_HERE = 4
SLOTS_OWN = 5
SLOTS = 20
ROWS_HERE = 48
ROW_TILES = 6
CHUNKS = 2 * ROW_TILES
SHARED = {10: 1, 11: -1}
GATHERS = CHUNKS + len(SHARED)
DIRECT = tuple(range(14))
SCHEDULE = (
    "c0", "o0", "n1", "h1", "z5", "z6", "h2", "z7", "z8", "c1", "o1", "h3", "z9", "z10", "s0", "c2",
    "o2", "z11", "z12", "s1", "z13", "z14", "c3", "o3", "s2", "c4", "o4", "s3", "c5", "o5", "s4",
    "c6", "o6", "c10", "c11", "s5", "c7", "o7", "s6", "c8", "o8", "r10", "s7", "c9", "o9", "r11",
    "mz", "s8", "o10", "o11", "my", "s9", "s10", "mx", "s11", "md",
)
Z_ORDER = [(0, 1)] + [(dz, dc) for dz in (7, 1, 6, 5, 4, 3, 2) for dc in (0, 1)]
X_ORDER = (2, 1, 3)
NEAR = 5
Y_ORDER = (2, 1, 3)


def block_of(out_ref, x, t, ct):
    rows = pl.ds(pl.multiple_of((x * ROW_TILES + t) * TILE, TILE), TILE)
    return out_ref.at[:, pl.ds(ct * TILE, TILE), rows]


def comm_kernel(w_hbm, place_ref, out_ref, maxima_ref, *scratch):
    ybufs = scratch[:GATHERS]
    (w_ref, w_sem, zbuf, staged, acc, zmax, ymax, xmax,
     z_send, z_recv, y_send, y_recv, x_send, x_recv, own_sem,
     sz_send, sz_recv, sy_send, sy_recv, sx_send, sx_recv, up_sem, down_sem) = scratch[GATHERS:]
    f = lax.axis_index("fsdp")
    y = lax.axis_index("group")
    x = f // NC
    c = f % NC
    z = c // 2
    core = c % 2

    def z_dev(step):
        dz, dc = step
        return 2 * ((z + dz) % NZ) + (core + dc) % 2

    def y_dev(dy):
        return (y + dy) % NY

    def x_dev(dx):
        return (x + dx) % NX

    fetch = pltpu.make_async_copy(w_hbm, w_ref, w_sem)
    fetch.start()
    barrier = pltpu.get_barrier_semaphore()
    for step in Z_ORDER[:NEAR]:
        pl.semaphore_signal(barrier, inc=1, device_id=(x * NC + z_dev(step), y), device_id_type=MESH)
    for d in Y_ORDER:
        pl.semaphore_signal(barrier, inc=1, device_id=(f, y_dev(d)), device_id_type=MESH)
    for d in X_ORDER:
        pl.semaphore_signal(barrier, inc=1, device_id=(x_dev(d) * NC + c, y), device_id_type=MESH)
    pl.semaphore_wait(barrier, NEAR + len(Y_ORDER) + len(X_ORDER))

    fetch.wait()
    waits = []

    def relay(level):
        if level:
            pl.semaphore_wait(up_sem.at[level - 1], 1)
            pl.semaphore_wait(down_sem.at[level - 1], 1)
        if level < 3:
            for dz, told in ((1, up_sem), (-1, down_sem)):
                pl.semaphore_signal(
                    told.at[level], inc=1, device_id=(x * NC + z_dev((dz, 0)), y), device_id_type=MESH
                )

    relay(0)
    def z_copy(k, ct):
        to = z_dev(Z_ORDER[k])
        cols = pl.ds(pl.multiple_of(to * (2 * TILE) + ct * TILE, TILE), TILE)
        rows = pl.ds(pl.multiple_of(c * ROWS_HERE, 16), ROWS_HERE)
        return pltpu.make_async_remote_copy(
            src_ref=w_ref.at[:, :, cols],
            dst_ref=zbuf.at[ct, :, rows, :],
            send_sem=z_send.at[ct, k],
            recv_sem=z_recv.at[ct, c],
            device_id=(x * NC + to, y),
            device_id_type=MESH,
        )

    def z_start(k, ct):
        copy = z_copy(k, ct)
        copy.start()
        waits.append(copy)

    for ct in range(2):
        cols = pl.ds(pl.multiple_of(c * (2 * TILE) + ct * TILE, TILE), TILE)
        rows = pl.ds(pl.multiple_of(c * ROWS_HERE, 16), ROWS_HERE)
        pltpu.make_async_copy(w_ref.at[:, :, cols], zbuf.at[ct, :, rows, :], z_recv.at[ct, c]).start()
    for k in range(5):
        z_start(k, 0)

    def z_wait(ct, first, last):
        def body(s, carry):
            rows = pl.ds(pl.multiple_of(s * ROWS_HERE, 16), ROWS_HERE)
            part = zbuf.at[ct, :, rows, :]
            pltpu.make_async_copy(part, part, z_recv.at[ct, s]).wait()
            return carry

        lax.fori_loop(first, last, body, 0)

    tile0 = (3 * z) // 4

    def tile_of(i):
        return (tile0 + i // 2) % ROW_TILES

    def first_source(t):
        return (8 * t) // 3

    def end_source(t):
        return (8 * t + 7) // 3 + 1

    acc[...] = jnp.zeros_like(acc)
    lane = lax.broadcasted_iota(jnp.int32, acc.shape, 1)
    sub = lax.broadcasted_iota(jnp.int32, acc.shape, 0)

    def shared_gather(i):
        return CHUNKS + sorted(SHARED).index(i)

    def experts_of(dy, first=0, count=EXPERTS_HERE):
        return pl.ds(y_dev(dy) * EXPERTS_HERE + first, count)

    def y_copy(g, n, to, experts):
        copy = pltpu.make_async_remote_copy(
            src_ref=ybufs[g].at[experts],
            dst_ref=ybufs[g].at[experts],
            send_sem=y_send.at[g, n],
            recv_sem=y_recv.at[g, n],
            device_id=(f, y_dev(to)),
            device_id_type=MESH,
        )
        copy.start()
        waits.append(copy)

    def y_wait(g, n, experts):
        part = ybufs[g].at[experts]
        pltpu.make_async_copy(part, part, y_recv.at[g, n]).wait()

    def y_spread(g):
        if g in DIRECT:
            y_copy(g, 2, 2, experts_of(0))
        y_copy(g, 0, 1, experts_of(0))
        y_copy(g, 1, -1, experts_of(0))

    def y_forward(g):
        if g in DIRECT:
            return
        y_wait(g, 0, experts_of(-1))
        y_copy(g, 2, 1, experts_of(-1, 0, 2))
        y_wait(g, 1, experts_of(1))
        y_copy(g, 3, -1, experts_of(1, 2, 2))

    def y_finish(g):
        if g in DIRECT:
            y_wait(g, 0, experts_of(-1))
            y_wait(g, 1, experts_of(1))
            y_wait(g, 2, experts_of(2))
        else:
            y_wait(g, 2, experts_of(2, 0, 2))
            y_wait(g, 3, experts_of(2, 2, 2))

    def share_copy(i):
        g = shared_gather(i)
        return pltpu.make_async_remote_copy(
            src_ref=ybufs[i].at[experts_of(0)],
            dst_ref=ybufs[g].at[experts_of(0)],
            send_sem=x_send.at[i, 2],
            recv_sem=x_recv.at[i, 2],
            device_id=(x_dev(SHARED[i]) * NC + c, y),
            device_id_type=MESH,
        )

    seen = set()

    def scale(i):
        order, ct = i // 2, i % 2
        t = tile_of(i)
        first, last = first_source(t), end_source(t)
        if ((order - 1) % ROW_TILES, ct) in seen:
            first = jnp.where(t > 0, jnp.maximum(first, end_source(t - 1)), first)
        if ((order + 1) % ROW_TILES, ct) in seen:
            last = jnp.where(t < ROW_TILES - 1, jnp.minimum(last, first_source(t + 1)), last)
        seen.add((order, ct))
        z_wait(ct, first, last)
        rows = pl.ds(pl.multiple_of(t * TILE, TILE), TILE)
        total = acc[...]
        for e in range(EXPERTS_HERE):
            block = zbuf[ct, e, rows, :].astype(jnp.float32)
            top = jnp.max(jnp.max(jnp.abs(block), axis=0, keepdims=True), axis=1, keepdims=True)
            code = (block / (top + EPSILON)).astype(jnp.bfloat16)
            ybufs[i][y * EXPERTS_HERE + e] = code.T
            at = (sub == t) & (lane == e * 32 + 2 * c + ct)
            total = jnp.where(at, top, total)
        acc[...] = total
        if i in SHARED:
            copy = share_copy(i)
            copy.start()
            waits.append(copy)

    def spread_shared(i):
        g = shared_gather(i)
        part = ybufs[g].at[experts_of(0)]
        pltpu.make_async_copy(part, part, x_recv.at[i, 2]).wait()
        y_spread(g)

    def select(i, n, g, owner):
        for j in range(SLOTS_OWN):
            expert = place_ref[0, owner * SLOTS_OWN + j]
            staged[i, n, j] = ybufs[g][expert]

    def x_copy(i, n, rows_of, owner):
        copy = pltpu.make_async_remote_copy(
            src_ref=staged.at[i, n],
            dst_ref=block_of(out_ref, rows_of, tile_of(i), i % 2),
            send_sem=x_send.at[i, n],
            recv_sem=x_recv.at[i, n],
            device_id=(owner * NC + c, y),
            device_id_type=MESH,
        )
        copy.start()
        waits.append(copy)

    def own_copy(i, n, k, rows_of):
        return pltpu.make_async_copy(
            staged.at[i, n], block_of(out_ref, rows_of, tile_of(i), i % 2), own_sem.at[i, k]
        )

    def select_and_send(i):
        y_finish(i)
        if i in SHARED:
            g, d = shared_gather(i), SHARED[i]
            select(i, 1, i, x_dev(-d))
            x_copy(i, 1, x, x_dev(-d))
            y_finish(g)
            select(i, 0, g, x_dev(d))
            x_copy(i, 0, x_dev(-d), x_dev(d))
            select(i, 2, i, x)
            own_copy(i, 2, 0, x).start()
            select(i, 3, g, x)
            own_copy(i, 3, 1, x_dev(-d)).start()
        else:
            for n, d in enumerate(X_ORDER):
                select(i, n, i, x_dev(d))
                x_copy(i, n, x, x_dev(d))
            select(i, 3, i, x)
            own_copy(i, 3, 0, x).start()

    def maxima_copy(ref, here, to, send, recv):
        return pltpu.make_async_remote_copy(
            src_ref=ref.at[here], dst_ref=ref.at[here], send_sem=send, recv_sem=recv,
            device_id=to, device_id_type=MESH,
        )

    def maxima_wait(ref, source, recv):
        part = ref.at[source]
        pltpu.make_async_copy(part, part, recv).wait()

    def maxima_z_send():
        zmax[c] = acc[...]
        for k, step in enumerate(Z_ORDER):
            copy = maxima_copy(zmax, c, (x * NC + z_dev(step), y), sz_send.at[k], sz_recv.at[c])
            copy.start()
            waits.append(copy)

    def maxima_y_send():
        for k, step in enumerate(Z_ORDER):
            maxima_wait(zmax, z_dev(step), sz_recv.at[z_dev(step)])
        ymax[y] = jnp.max(zmax[...], axis=0)
        for n, d in enumerate(Y_ORDER):
            copy = maxima_copy(ymax, y, (f, y_dev(d)), sy_send.at[n], sy_recv.at[n])
            copy.start()
            waits.append(copy)

    def maxima_x_send():
        for n, d in enumerate(Y_ORDER):
            maxima_wait(ymax, (y - d) % NY, sy_recv.at[n])
        xmax[x] = ymax[...]
        for n, d in enumerate(X_ORDER):
            copy = maxima_copy(xmax, x, (x_dev(d) * NC + c, y), sx_send.at[n], sx_recv.at[n])
            copy.start()
            waits.append(copy)

    def maxima_done():
        for n, d in enumerate(X_ORDER):
            maxima_wait(xmax, (x - d) % NX, sx_recv.at[n])
        maxima_ref[...] = xmax[...]

    for step in SCHEDULE:
        if step == "mz":
            maxima_z_send()
        elif step == "my":
            maxima_y_send()
        elif step == "mx":
            maxima_x_send()
        elif step == "md":
            maxima_done()
        else:
            act, i = step[0], int(step[1:])
            if act == "h":
                relay(i)
            elif act == "n":
                for k in range(5):
                    z_start(k, 1)
            elif act == "z":
                for ct in range(2):
                    z_start(i, ct)
            elif act == "c":
                scale(i)
            elif act == "o":
                y_spread(i)
            elif act == "r":
                spread_shared(i)
            elif act == "f":
                y_forward(i)
            elif act == "g":
                y_forward(shared_gather(i))
            else:
                select_and_send(i)

    for copy in waits:
        copy.wait_send()
    def x_wait(i, n, rows_of):
        part = block_of(out_ref, rows_of, tile_of(i), i % 2)
        pltpu.make_async_copy(part, part, x_recv.at[i, n]).wait()

    for i in range(CHUNKS):
        if i in SHARED:
            d = SHARED[i]
            x_wait(i, 1, x_dev(d))
            x_wait(i, 0, x_dev(2))
            own_copy(i, 2, 0, x).wait()
            own_copy(i, 3, 1, x_dev(-d)).wait()
        else:
            for n, d in enumerate(X_ORDER):
                x_wait(i, n, x_dev(-d))
            own_copy(i, 3, 0, x).wait()


def exchange(weights, placement):
    sem = pltpu.SemaphoreType.DMA
    return pl.pallas_call(
        comm_kernel,
        out_shape=(
            pltpu.VMEM((SLOTS_OWN, 2 * TILE, NX * ROW_TILES * TILE), jnp.bfloat16),
            pltpu.VMEM((NX, NY, 8, TILE), jnp.float32),
        ),
        in_specs=[pl.BlockSpec(memory_space=pltpu.HBM), pl.BlockSpec(memory_space=pltpu.SMEM)],
        out_specs=(pl.BlockSpec(memory_space=pltpu.VMEM), pl.BlockSpec(memory_space=pltpu.VMEM)),
        scratch_shapes=[pltpu.VMEM((16, TILE, TILE), jnp.bfloat16)] * GATHERS
        + [
            pltpu.VMEM((EXPERTS_HERE, ROWS_HERE, 2 * TILE * NC), jnp.bfloat16),
            sem,
            pltpu.VMEM((2, EXPERTS_HERE, ROW_TILES * TILE, TILE), jnp.bfloat16),
            pltpu.VMEM((CHUNKS, 4, SLOTS_OWN, TILE, TILE), jnp.bfloat16),
            pltpu.VMEM((8, TILE), jnp.float32),
            pltpu.VMEM((NC, 8, TILE), jnp.float32),
            pltpu.VMEM((NY, 8, TILE), jnp.float32),
            pltpu.VMEM((NX, NY, 8, TILE), jnp.float32),
            sem((2, 15)), sem((2, NC)),
            sem((GATHERS, 4)), sem((GATHERS, 4)),
            sem((CHUNKS, 3)), sem((CHUNKS, 3)), sem((CHUNKS, 2)),
            sem((15,)), sem((NC,)),
            sem((3,)), sem((3,)),
            sem((3,)), sem((3,)),
            pltpu.SemaphoreType.REGULAR((3,)), pltpu.SemaphoreType.REGULAR((3,)),
        ],
        compiler_params=pltpu.CompilerParams(
            collective_id=0, has_side_effects=True, vmem_limit_bytes=40 * 2**20
        ),
        name="reshard",
    )(weights, placement)


PIECES = 8


def finish_kernel(place_ref, codes_ref, maxima_ref, out_ref, scales_ref, sems):
    rows = 2 * TILE // PIECES
    copies = []
    for q in range(PIECES):
        part = pl.ds(q * rows, rows)
        copy = pltpu.make_async_copy(codes_ref.at[:, part], out_ref.at[:, part], sems.at[q])
        copy.start()
        copies.append(copy)
    for s in range(SLOTS):
        expert = place_ref[0, s]
        which = expert % EXPERTS_HERE
        table = maxima_ref[:, expert // EXPERTS_HERE]
        part = table[:, :, :32]
        for e in range(1, EXPERTS_HERE):
            part = jnp.where(which == e, table[:, :, 32 * e:32 * (e + 1)], part)
        for q in range(NX):
            scales_ref[0, s, ROW_TILES * q:ROW_TILES * (q + 1), :] = part[q, :ROW_TILES]
    for copy in copies:
        copy.wait()


def finish(placement, codes, maxima):
    return pl.pallas_call(
        finish_kernel,
        out_shape=(
            jax.ShapeDtypeStruct(codes.shape, codes.dtype),
            jax.ShapeDtypeStruct((1, SLOTS, NX * ROW_TILES, 32), jnp.float32),
        ),
        in_specs=[
            pl.BlockSpec(memory_space=pltpu.SMEM),
            pl.BlockSpec(memory_space=pl.ANY),
            pl.BlockSpec(memory_space=pltpu.VMEM),
        ],
        out_specs=(pl.BlockSpec(memory_space=pl.ANY), pl.BlockSpec(memory_space=pltpu.VMEM)),
        scratch_shapes=[pltpu.SemaphoreType.DMA((PIECES,))],
        compiler_params=pltpu.CompilerParams(vmem_limit_bytes=16 * 2**20),
        name="finish",
    )(placement, codes, maxima)


def on_device(weights, placement):
    weights = pltpu.with_memory_space_constraint(weights, pltpu.HBM)
    placement = pltpu.with_memory_space_constraint(placement, pltpu.HBM)
    codes, maxima = exchange(weights, placement)
    codes, scales = finish(placement, codes, maxima)
    return jnp.transpose(codes, (1, 0, 2))[None], scales


def solution(mesh):
    in_specs = (P("group", "fsdp", None), P("group", None))
    out_specs = (P("group", "fsdp", None, None), P("group", None, None, None))
    return jax.shard_map(
        on_device, mesh=mesh, in_specs=in_specs, out_specs=out_specs, check_vma=False
    )
```

```python
import jax
import jax.numpy as jnp
from jax import lax
from jax.experimental import pallas as pl
from jax.experimental.pallas import tpu as pltpu
from jax.sharding import PartitionSpec as P

MESH = pl.DeviceIdType.MESH
TILE = 128
EPSILON = 1e-6
NX, NY, NZ = 4, 4, 8
NC = 16
EXPERTS_HERE = 4
SLOTS_OWN = 5
SLOTS = 20
ROWS_HERE = 48
ROW_TILES = 6
CHUNKS = 2 * ROW_TILES
SHARED = {10: 1, 11: -1}
GATHERS = CHUNKS + len(SHARED)
DIRECT = tuple(range(14))
SCHEDULE = (
    "c0", "o0", "n1", "h1", "z5", "z6", "h2", "z7", "z8", "c1", "o1", "h3", "z9", "z10", "z11",
    "z12", "z13", "z14", "s0", "c2", "o2", "s1", "c3", "o3", "s2", "c4", "o4", "s3", "c5", "o5",
    "s4", "c10", "c11", "c6", "o6", "s5", "c7", "o7", "s6", "c8", "o8", "r10", "s7", "c9", "o9",
    "r11", "mz", "s8", "o10", "o11", "my", "s9", "s10", "mx", "s11", "md",
)
Z_ORDER = [(0, 1)] + [(dz, dc) for dz in (7, 1, 6, 5, 4, 3, 2) for dc in (0, 1)]
X_ORDER = (2, 1, 3)
NEAR = 5
Y_ORDER = (2, 1, 3)


def block_of(out_ref, x, t, ct):
    rows = pl.ds(pl.multiple_of((x * ROW_TILES + t) * TILE, TILE), TILE)
    return out_ref.at[:, pl.ds(ct * TILE, TILE), rows]


def comm_kernel(w_hbm, place_ref, out_ref, maxima_ref, *scratch):
    ybufs = scratch[:GATHERS]
    (w_ref, w_sem, zbuf, staged, acc, zmax, ymax, xmax,
     z_send, z_recv, y_send, y_recv, x_send, x_recv, own_sem,
     sz_send, sz_recv, sy_send, sy_recv, sx_send, sx_recv, up_sem, down_sem) = scratch[GATHERS:]
    f = lax.axis_index("fsdp")
    y = lax.axis_index("group")
    x = f // NC
    c = f % NC
    z = c // 2
    core = c % 2

    def z_dev(step):
        dz, dc = step
        return 2 * ((z + dz) % NZ) + (core + dc) % 2

    def y_dev(dy):
        return (y + dy) % NY

    def x_dev(dx):
        return (x + dx) % NX

    fetch = pltpu.make_async_copy(w_hbm, w_ref, w_sem)
    fetch.start()
    barrier = pltpu.get_barrier_semaphore()
    for step in Z_ORDER[:NEAR]:
        pl.semaphore_signal(barrier, inc=1, device_id=(x * NC + z_dev(step), y), device_id_type=MESH)
    for d in Y_ORDER:
        pl.semaphore_signal(barrier, inc=1, device_id=(f, y_dev(d)), device_id_type=MESH)
    for d in X_ORDER:
        pl.semaphore_signal(barrier, inc=1, device_id=(x_dev(d) * NC + c, y), device_id_type=MESH)
    pl.semaphore_wait(barrier, NEAR + len(Y_ORDER) + len(X_ORDER))

    fetch.wait()
    waits = []

    def relay(level):
        if level:
            pl.semaphore_wait(up_sem.at[level - 1], 1)
            pl.semaphore_wait(down_sem.at[level - 1], 1)
        if level < 3:
            for dz, told in ((1, up_sem), (-1, down_sem)):
                pl.semaphore_signal(
                    told.at[level], inc=1, device_id=(x * NC + z_dev((dz, 0)), y), device_id_type=MESH
                )

    relay(0)
    def z_copy(k, ct):
        to = z_dev(Z_ORDER[k])
        cols = pl.ds(pl.multiple_of(to * (2 * TILE) + ct * TILE, TILE), TILE)
        rows = pl.ds(pl.multiple_of(c * ROWS_HERE, 16), ROWS_HERE)
        return pltpu.make_async_remote_copy(
            src_ref=w_ref.at[:, :, cols],
            dst_ref=zbuf.at[ct, :, rows, :],
            send_sem=z_send.at[ct, k],
            recv_sem=z_recv.at[ct, c],
            device_id=(x * NC + to, y),
            device_id_type=MESH,
        )

    def z_start(k, ct):
        copy = z_copy(k, ct)
        copy.start()
        waits.append(copy)

    for ct in range(2):
        cols = pl.ds(pl.multiple_of(c * (2 * TILE) + ct * TILE, TILE), TILE)
        rows = pl.ds(pl.multiple_of(c * ROWS_HERE, 16), ROWS_HERE)
        pltpu.make_async_copy(w_ref.at[:, :, cols], zbuf.at[ct, :, rows, :], z_recv.at[ct, c]).start()
    for k in range(5):
        z_start(k, 0)

    def z_wait(ct, first, last):
        def body(s, carry):
            rows = pl.ds(pl.multiple_of(s * ROWS_HERE, 16), ROWS_HERE)
            part = zbuf.at[ct, :, rows, :]
            pltpu.make_async_copy(part, part, z_recv.at[ct, s]).wait()
            return carry

        lax.fori_loop(first, last, body, 0)

    tile0 = (3 * z) // 4

    def tile_of(i):
        return (tile0 + i // 2) % ROW_TILES

    def first_source(t):
        return (8 * t) // 3

    def end_source(t):
        return (8 * t + 7) // 3 + 1

    acc[...] = jnp.zeros_like(acc)
    lane = lax.broadcasted_iota(jnp.int32, acc.shape, 1)
    sub = lax.broadcasted_iota(jnp.int32, acc.shape, 0)

    def shared_gather(i):
        return CHUNKS + sorted(SHARED).index(i)

    def experts_of(dy, first=0, count=EXPERTS_HERE):
        return pl.ds(y_dev(dy) * EXPERTS_HERE + first, count)

    def y_copy(g, n, to, experts):
        copy = pltpu.make_async_remote_copy(
            src_ref=ybufs[g].at[experts],
            dst_ref=ybufs[g].at[experts],
            send_sem=y_send.at[g, n],
            recv_sem=y_recv.at[g, n],
            device_id=(f, y_dev(to)),
            device_id_type=MESH,
        )
        copy.start()
        waits.append(copy)

    def y_wait(g, n, experts):
        part = ybufs[g].at[experts]
        pltpu.make_async_copy(part, part, y_recv.at[g, n]).wait()

    def y_spread(g):
        if g in DIRECT:
            y_copy(g, 2, 2, experts_of(0))
        y_copy(g, 0, 1, experts_of(0))
        y_copy(g, 1, -1, experts_of(0))

    def y_forward(g):
        if g in DIRECT:
            return
        y_wait(g, 0, experts_of(-1))
        y_copy(g, 2, 1, experts_of(-1, 0, 2))
        y_wait(g, 1, experts_of(1))
        y_copy(g, 3, -1, experts_of(1, 2, 2))

    def y_finish(g):
        if g in DIRECT:
            y_wait(g, 0, experts_of(-1))
            y_wait(g, 1, experts_of(1))
            y_wait(g, 2, experts_of(2))
        else:
            y_wait(g, 2, experts_of(2, 0, 2))
            y_wait(g, 3, experts_of(2, 2, 2))

    def share_copy(i):
        g = shared_gather(i)
        return pltpu.make_async_remote_copy(
            src_ref=ybufs[i].at[experts_of(0)],
            dst_ref=ybufs[g].at[experts_of(0)],
            send_sem=x_send.at[i, 2],
            recv_sem=x_recv.at[i, 2],
            device_id=(x_dev(SHARED[i]) * NC + c, y),
            device_id_type=MESH,
        )

    seen = set()

    def scale(i):
        order, ct = i // 2, i % 2
        t = tile_of(i)
        first, last = first_source(t), end_source(t)
        if ((order - 1) % ROW_TILES, ct) in seen:
            first = jnp.where(t > 0, jnp.maximum(first, end_source(t - 1)), first)
        if ((order + 1) % ROW_TILES, ct) in seen:
            last = jnp.where(t < ROW_TILES - 1, jnp.minimum(last, first_source(t + 1)), last)
        seen.add((order, ct))
        z_wait(ct, first, last)
        rows = pl.ds(pl.multiple_of(t * TILE, TILE), TILE)
        total = acc[...]
        for e in range(EXPERTS_HERE):
            block = zbuf[ct, e, rows, :].astype(jnp.float32)
            top = jnp.max(jnp.max(jnp.abs(block), axis=0, keepdims=True), axis=1, keepdims=True)
            code = (block / (top + EPSILON)).astype(jnp.bfloat16)
            ybufs[i][y * EXPERTS_HERE + e] = code.T
            at = (sub == t) & (lane == e * 32 + 2 * c + ct)
            total = jnp.where(at, top, total)
        acc[...] = total
        if i in SHARED:
            copy = share_copy(i)
            copy.start()
            waits.append(copy)

    def spread_shared(i):
        g = shared_gather(i)
        part = ybufs[g].at[experts_of(0)]
        pltpu.make_async_copy(part, part, x_recv.at[i, 2]).wait()
        y_spread(g)

    def select(i, n, g, owner):
        for j in range(SLOTS_OWN):
            expert = place_ref[0, owner * SLOTS_OWN + j]
            staged[i, n, j] = ybufs[g][expert]

    def x_copy(i, n, rows_of, owner):
        copy = pltpu.make_async_remote_copy(
            src_ref=staged.at[i, n],
            dst_ref=block_of(out_ref, rows_of, tile_of(i), i % 2),
            send_sem=x_send.at[i, n],
            recv_sem=x_recv.at[i, n],
            device_id=(owner * NC + c, y),
            device_id_type=MESH,
        )
        copy.start()
        waits.append(copy)

    def own_copy(i, n, k, rows_of):
        return pltpu.make_async_copy(
            staged.at[i, n], block_of(out_ref, rows_of, tile_of(i), i % 2), own_sem.at[i, k]
        )

    def select_and_send(i):
        y_finish(i)
        if i in SHARED:
            g, d = shared_gather(i), SHARED[i]
            select(i, 1, i, x_dev(-d))
            x_copy(i, 1, x, x_dev(-d))
            y_finish(g)
            select(i, 0, g, x_dev(d))
            x_copy(i, 0, x_dev(-d), x_dev(d))
            select(i, 2, i, x)
            own_copy(i, 2, 0, x).start()
            select(i, 3, g, x)
            own_copy(i, 3, 1, x_dev(-d)).start()
        else:
            for n, d in enumerate(X_ORDER):
                select(i, n, i, x_dev(d))
                x_copy(i, n, x, x_dev(d))
            select(i, 3, i, x)
            own_copy(i, 3, 0, x).start()

    def maxima_copy(ref, here, to, send, recv):
        return pltpu.make_async_remote_copy(
            src_ref=ref.at[here], dst_ref=ref.at[here], send_sem=send, recv_sem=recv,
            device_id=to, device_id_type=MESH,
        )

    def maxima_wait(ref, source, recv):
        part = ref.at[source]
        pltpu.make_async_copy(part, part, recv).wait()

    def maxima_z_send():
        zmax[c] = acc[...]
        for k, step in enumerate(Z_ORDER):
            copy = maxima_copy(zmax, c, (x * NC + z_dev(step), y), sz_send.at[k], sz_recv.at[c])
            copy.start()
            waits.append(copy)

    def maxima_y_send():
        for k, step in enumerate(Z_ORDER):
            maxima_wait(zmax, z_dev(step), sz_recv.at[z_dev(step)])
        ymax[y] = jnp.max(zmax[...], axis=0)
        for n, d in enumerate(Y_ORDER):
            copy = maxima_copy(ymax, y, (f, y_dev(d)), sy_send.at[n], sy_recv.at[n])
            copy.start()
            waits.append(copy)

    def maxima_x_send():
        for n, d in enumerate(Y_ORDER):
            maxima_wait(ymax, (y - d) % NY, sy_recv.at[n])
        xmax[x] = ymax[...]
        for n, d in enumerate(X_ORDER):
            copy = maxima_copy(xmax, x, (x_dev(d) * NC + c, y), sx_send.at[n], sx_recv.at[n])
            copy.start()
            waits.append(copy)

    def maxima_done():
        for n, d in enumerate(X_ORDER):
            maxima_wait(xmax, (x - d) % NX, sx_recv.at[n])
        maxima_ref[...] = xmax[...]

    for step in SCHEDULE:
        if step == "mz":
            maxima_z_send()
        elif step == "my":
            maxima_y_send()
        elif step == "mx":
            maxima_x_send()
        elif step == "md":
            maxima_done()
        else:
            act, i = step[0], int(step[1:])
            if act == "h":
                relay(i)
            elif act == "n":
                for k in range(5):
                    z_start(k, 1)
            elif act == "z":
                for ct in range(2):
                    z_start(i, ct)
            elif act == "c":
                scale(i)
            elif act == "o":
                y_spread(i)
            elif act == "r":
                spread_shared(i)
            elif act == "f":
                y_forward(i)
            elif act == "g":
                y_forward(shared_gather(i))
            else:
                select_and_send(i)

    for copy in waits:
        copy.wait_send()
    def x_wait(i, n, rows_of):
        part = block_of(out_ref, rows_of, tile_of(i), i % 2)
        pltpu.make_async_copy(part, part, x_recv.at[i, n]).wait()

    for i in range(CHUNKS):
        if i in SHARED:
            d = SHARED[i]
            x_wait(i, 1, x_dev(d))
            x_wait(i, 0, x_dev(2))
            own_copy(i, 2, 0, x).wait()
            own_copy(i, 3, 1, x_dev(-d)).wait()
        else:
            for n, d in enumerate(X_ORDER):
                x_wait(i, n, x_dev(-d))
            own_copy(i, 3, 0, x).wait()


def exchange(weights, placement):
    sem = pltpu.SemaphoreType.DMA
    return pl.pallas_call(
        comm_kernel,
        out_shape=(
            pltpu.VMEM((SLOTS_OWN, 2 * TILE, NX * ROW_TILES * TILE), jnp.bfloat16),
            pltpu.VMEM((NX, NY, 8, TILE), jnp.float32),
        ),
        in_specs=[pl.BlockSpec(memory_space=pltpu.HBM), pl.BlockSpec(memory_space=pltpu.SMEM)],
        out_specs=(pl.BlockSpec(memory_space=pltpu.VMEM), pl.BlockSpec(memory_space=pltpu.VMEM)),
        scratch_shapes=[pltpu.VMEM((16, TILE, TILE), jnp.bfloat16)] * GATHERS
        + [
            pltpu.VMEM((EXPERTS_HERE, ROWS_HERE, 2 * TILE * NC), jnp.bfloat16),
            sem,
            pltpu.VMEM((2, EXPERTS_HERE, ROW_TILES * TILE, TILE), jnp.bfloat16),
            pltpu.VMEM((CHUNKS, 4, SLOTS_OWN, TILE, TILE), jnp.bfloat16),
            pltpu.VMEM((8, TILE), jnp.float32),
            pltpu.VMEM((NC, 8, TILE), jnp.float32),
            pltpu.VMEM((NY, 8, TILE), jnp.float32),
            pltpu.VMEM((NX, NY, 8, TILE), jnp.float32),
            sem((2, 15)), sem((2, NC)),
            sem((GATHERS, 4)), sem((GATHERS, 4)),
            sem((CHUNKS, 3)), sem((CHUNKS, 3)), sem((CHUNKS, 2)),
            sem((15,)), sem((NC,)),
            sem((3,)), sem((3,)),
            sem((3,)), sem((3,)),
            pltpu.SemaphoreType.REGULAR((3,)), pltpu.SemaphoreType.REGULAR((3,)),
        ],
        compiler_params=pltpu.CompilerParams(
            collective_id=0, has_side_effects=True, vmem_limit_bytes=40 * 2**20
        ),
        name="reshard",
    )(weights, placement)


PIECES = 8


def finish_kernel(place_ref, codes_ref, maxima_ref, out_ref, scales_ref, sems):
    rows = 2 * TILE // PIECES
    copies = []
    for q in range(PIECES):
        part = pl.ds(q * rows, rows)
        copy = pltpu.make_async_copy(codes_ref.at[:, part], out_ref.at[:, part], sems.at[q])
        copy.start()
        copies.append(copy)
    for s in range(SLOTS):
        expert = place_ref[0, s]
        which = expert % EXPERTS_HERE
        table = maxima_ref[:, expert // EXPERTS_HERE]
        part = table[:, :, :32]
        for e in range(1, EXPERTS_HERE):
            part = jnp.where(which == e, table[:, :, 32 * e:32 * (e + 1)], part)
        for q in range(NX):
            scales_ref[0, s, ROW_TILES * q:ROW_TILES * (q + 1), :] = part[q, :ROW_TILES]
    for copy in copies:
        copy.wait()


def finish(placement, codes, maxima):
    return pl.pallas_call(
        finish_kernel,
        out_shape=(
            jax.ShapeDtypeStruct(codes.shape, codes.dtype),
            jax.ShapeDtypeStruct((1, SLOTS, NX * ROW_TILES, 32), jnp.float32),
        ),
        in_specs=[
            pl.BlockSpec(memory_space=pltpu.SMEM),
            pl.BlockSpec(memory_space=pl.ANY),
            pl.BlockSpec(memory_space=pltpu.VMEM),
        ],
        out_specs=(pl.BlockSpec(memory_space=pl.ANY), pl.BlockSpec(memory_space=pltpu.VMEM)),
        scratch_shapes=[pltpu.SemaphoreType.DMA((PIECES,))],
        compiler_params=pltpu.CompilerParams(vmem_limit_bytes=16 * 2**20),
        name="finish",
    )(placement, codes, maxima)


def on_device(weights, placement):
    weights = pltpu.with_memory_space_constraint(weights, pltpu.HBM)
    placement = pltpu.with_memory_space_constraint(placement, pltpu.HBM)
    codes, maxima = exchange(weights, placement)
    codes, scales = finish(placement, codes, maxima)
    return jnp.transpose(codes, (1, 0, 2))[None], scales


def solution(mesh):
    in_specs = (P("group", "fsdp", None), P("group", None))
    out_specs = (P("group", "fsdp", None, None), P("group", None, None, None))
    return jax.shard_map(
        on_device, mesh=mesh, in_specs=in_specs, out_specs=out_specs, check_vma=False
    )
```
